32 devices in a mesh: groups: 2 (over y), col: 4 (over x, core), row: 4 (over z).
Axes of the slice: x: 2, y: 2, z: 4, core: 2. Of those that a mesh axis runs over, the one named last changes fastest.
Arguments:
- right_vectors: bfloat16 [128, 32768], P('groups', ('col', 'row')), parts along dimension 0, may hold values from -6 to 6
- left_vectors: bfloat16 [128, 8192], P('groups', ('row', 'col')), parts along dimension 0, may hold values from -6 to 6
- diag_tiles: bfloat16 [16384, 2048], P(('groups', 'row', 'col')), parts along dimension 0, may hold values from -0.125 to 0.125
- tile_ranks: int32 [8, 16], P('groups', 'col'), parts along dimension 0, may hold values from 20 to 400, as said below
- tile_order: int32 [8, 16], P(('groups', 'col')), parts along dimension 0, may hold values from 0 to 15, each once within a row
- v_panels: bfloat16 [320, 128, 2048], P(('groups', 'col', 'row')), parts along dimension 0, may hold values from -0.25 to 0.25
- u_panels: bfloat16 [320, 128, 2048], P(('groups', 'col', 'row')), parts along dimension 0, may hold values from -0.1875 to 0.1875
Outputs:
- product_rows: bfloat16 [128, 8192], P('groups', ('row', 'col')), parts along dimension 0
- product_cols: bfloat16 [128, 32768], P('groups', ('col', 'row')), parts along dimension 0
The draws below stay inside these ranges and needn't reach their ends.
There are 2 independent parts, one for each index of `groups`. The reference program is written for one: setup_inputs(seed, part) draws one part's arguments, and reference() takes and returns one part's arrays. A program takes and returns all parts, laid end to end along the dimension named above; each array names one. Nothing has to cross between parts.
Inputs may be any that keep to these rules, and one draw needn't show every extreme that they name: `tile_ranks`: in every column group the off-diagonal tiles together need at most 40 panels; entries of diagonal tiles are not read. `tile_order`: each row lists the 16 positions of one group once.
All inputs are finite; a program needn't handle non-finite values.
Results may differ from the reference program's by a relative error of at most 0.005.
Values may be sent and summed in bfloat16 or wider, within the bound.
A program may use at most 128 MiB of HBM per device.

```python
import jax
import jax.numpy as jnp
from jax import lax

TILE = 2048
VECS = 64
PANEL = 128
RANK_MAX = 400
RANK_MIN = 20
TCOL_DEV = 4
SLOTS_DEV = 10
TROWS = 4
TCOLS = 16
N_COL = 4
N_ROW = 4


def draw_tile_ranks(key, part):
    key = jax.random.fold_in(key, 7)
    row_total = N_ROW
    col_total = TCOL_DEV * N_COL
    row_ids = jnp.arange(row_total, dtype=jnp.int32)[:, None]
    col_ids = jnp.arange(col_total, dtype=jnp.int32)[None, :]
    distance = jnp.abs(row_ids - col_ids)
    ceiling_rank = jnp.minimum(2 * RANK_MAX // (distance + 1), RANK_MAX)
    spread = jnp.maximum(ceiling_rank - RANK_MIN + 1, 1)
    noise = jax.random.randint(key, (row_total, col_total), 0, 1 << 20, dtype=jnp.int32) % spread
    noise = jnp.where(distance >= 2, noise, 0)
    raw_ranks = jnp.maximum(ceiling_rank - noise, RANK_MIN).astype(jnp.int32)
    tile_count = row_total * TCOL_DEV
    grouped = raw_ranks.reshape(row_total, N_COL, TCOL_DEV).transpose(1, 0, 2).reshape(N_COL, tile_count)
    on_diagonal = (distance == 0).reshape(row_total, N_COL, TCOL_DEV).transpose(1, 0, 2).reshape(N_COL, tile_count)
    needed = jnp.where(on_diagonal, 0, (grouped + PANEL - 1) // PANEL).astype(jnp.int32)
    off_diag = jnp.where(on_diagonal, 0, 1).astype(jnp.int32)
    after_count = (jnp.sum(off_diag, axis=1, keepdims=True) - jnp.cumsum(off_diag, axis=1)).astype(jnp.int32)
    capacity = N_ROW * SLOTS_DEV

    def fill_step(used_slots, pair_item):
        need_now, rest_now = pair_item
        allowed_now = jnp.minimum(need_now, capacity - used_slots - rest_now).astype(jnp.int32)
        return ((used_slots + allowed_now).astype(jnp.int32), allowed_now)
    final_used, allowed = lax.scan(fill_step, jnp.zeros((N_COL,), jnp.int32), (needed.T, after_count.T))
    clipped = jnp.where(on_diagonal, grouped, jnp.minimum(grouped, allowed.T * PANEL))
    return clipped.reshape(N_COL, row_total, TCOL_DEV).transpose(1, 0, 2).reshape(row_total, col_total).astype(jnp.int32)


def spiked(drawn, rng, source, target, blocks, factor):
    owner, partner = [(jnp.arange(drawn.shape[axis_at]) // (drawn.shape[axis_at] // blocks)).reshape([-1 if axis == axis_at else 1 for axis in range(drawn.ndim)]) for axis_at in (source, target)]
    chosen = jax.random.permutation(rng, blocks)[partner]
    strong = (owner == chosen) | (owner == (partner + blocks // 2) % blocks)
    return jnp.where(strong, factor * drawn, drawn)


def level_of(key, extent, cuts, low, top_value):
    def one(position, blocks):
        heights = jax.random.uniform(jax.random.fold_in(jax.random.fold_in(key, 6), position), (blocks,), jnp.float32, low / len(cuts), top_value / len(cuts))
        return jnp.repeat(jnp.exp(heights), extent[position] // blocks).reshape((-1,) + (1,) * (len(extent) - position - 1))

    factor_of = one(*cuts[0])
    for cut in cuts[1:]:
        factor_of = factor_of * one(*cut)
    return factor_of


def normal_values(stream_key, shape, scale, reach, split=(), kind=jnp.bfloat16):
    result = jax.random.normal(stream_key, shape, jnp.float32) * scale
    if len(split) > 0:
        result = level_of(stream_key, shape, split, -0.22, 0.18) * result
    return jnp.clip(result, min=-reach, max=reach).astype(kind)


def gaussian_with(stream_key, dims, width, most, shards, heavy, kind=jnp.bfloat16):
    values = width * jax.random.normal(stream_key, dims, jnp.float32)
    if shards:
        values = values * level_of(stream_key, dims, shards, -0.22, 0.18)
    return jnp.clip(spiked(values, jax.random.fold_in(stream_key, 3), *heavy), -most, most).astype(kind)


def setup_inputs(seed: int = 0, part: int = 0) -> dict:
    streams_of = jax.random.split(jax.random.key(seed), 8)
    part_splits = jax.random.split(jax.random.fold_in(streams_of[7], part), 8)
    right_vectors = normal_values(part_splits[0], (VECS, TCOLS * TILE), 1.0, 6.0, ((1, 16),))
    left_vectors = normal_values(part_splits[1], (VECS, TROWS * TILE), 1.0, 6.0, ((1, 16),))
    diag_tiles = normal_values(part_splits[2], (TROWS * TILE, TILE), TILE ** -0.5, 0.125, ((0, 16),))
    tile_ranks = draw_tile_ranks(jax.random.fold_in(jax.random.fold_in(streams_of[7], part), 71), part)
    tile_order = jax.vmap(lambda own: jax.random.permutation(own, TROWS * TCOL_DEV))(jax.random.split(part_splits[4], N_COL)).reshape((N_COL, TROWS * TCOL_DEV)).astype(jnp.int32)
    v_panels = normal_values(part_splits[5], (N_COL * N_ROW * SLOTS_DEV, PANEL, TILE), (TILE // 4) ** -0.5, 0.25, ((0, 16),))
    u_panels = gaussian_with(part_splits[6], (N_COL * N_ROW * SLOTS_DEV, PANEL, TILE), TILE ** -0.5, 0.1875, ((0, 16),), (0, 2, 16, 2.0))
    return {"right_vectors": right_vectors, "left_vectors": left_vectors, "diag_tiles": diag_tiles, "tile_ranks": tile_ranks, "tile_order": tile_order, "v_panels": v_panels, "u_panels": u_panels}


def panel_layout(ranks_group, order_group, group_index, helper, slot_count, row_count):
    per_group = ranks_group.shape[1]
    tile_count = row_count * per_group
    positions = jnp.arange(tile_count, dtype=jnp.int32)
    tile_rows = positions // per_group
    tile_cols = positions % per_group
    on_diagonal = tile_rows == group_index * per_group + tile_cols
    flat_ranks = ranks_group.reshape(tile_count).astype(jnp.int32)
    needed = jnp.where(on_diagonal, 0, (flat_ranks + PANEL - 1) // PANEL).astype(jnp.int32)
    listing = (order_group.astype(jnp.int32)[:, None] == positions[None, :]).astype(jnp.int32)
    listed = jnp.sum(listing * needed[None, :], axis=1).astype(jnp.int32)
    starts = (jnp.cumsum(listed) - listed).astype(jnp.int32)
    slot_ids = (helper * slot_count + jnp.arange(slot_count, dtype=jnp.int32)).astype(jnp.int32)
    inside = ((slot_ids[:, None] >= starts[None, :]) & (slot_ids[:, None] < (starts + listed)[None, :])).astype(jnp.int32)
    tile_hot = jnp.sum(inside[:, :, None] * listing[None, :, :], axis=1).astype(jnp.int32)
    panel_number = (slot_ids - jnp.sum(inside * starts[None, :], axis=1)).astype(jnp.int32)
    slot_ranks = jnp.sum(tile_hot * flat_ranks[None, :], axis=1).astype(jnp.int32)
    widths = jnp.clip(slot_ranks - panel_number * PANEL, 0, PANEL)
    valid_mask = (jnp.arange(PANEL, dtype=jnp.int32)[None, :] < widths[:, None]).astype(jnp.float32)
    shaped = tile_hot.reshape(slot_count, row_count, per_group)
    row_hot = jnp.sum(shaped, axis=2).astype(jnp.float32)
    col_hot = jnp.sum(shaped, axis=1).astype(jnp.float32)
    return row_hot, col_hot, valid_mask


def reference(right_vectors, left_vectors, diag_tiles, tile_ranks, tile_order, v_panels, u_panels):
    highest = lax.Precision.HIGHEST
    row_count = N_ROW
    col_count = N_COL
    per_group = TCOL_DEV
    group_slots = SLOTS_DEV * N_ROW
    x_blocks = right_vectors.astype(jnp.float32).reshape(VECS, col_count, per_group, TILE)
    w_blocks = left_vectors.astype(jnp.float32).reshape(VECS, row_count, TILE)
    v_groups = v_panels.reshape(col_count, group_slots, PANEL, TILE)
    u_groups = u_panels.reshape(col_count, group_slots, PANEL, TILE)
    row_total = jnp.zeros((row_count, VECS, TILE), jnp.float32)
    column_parts = []
    for column_group in range(col_count):
        ranks_here = tile_ranks[:, column_group * per_group:(column_group + 1) * per_group]
        row_hot, col_hot, valid_mask = panel_layout(ranks_here, tile_order[column_group], column_group, 0, group_slots, row_count)
        v_here = v_groups[column_group].astype(jnp.float32)
        u_here = u_groups[column_group].astype(jnp.float32)
        picked_x = jnp.einsum("pb,vbn->pvn", col_hot, x_blocks[:, column_group], precision=highest)
        coefficients = jnp.einsum("pkn,pvn->pvk", v_here, picked_x, precision=highest) * valid_mask[:, None, :]
        coefficients = lax.optimization_barrier(coefficients.astype(jnp.bfloat16)).astype(jnp.float32)
        products = jnp.einsum("pvk,pkn->pvn", coefficients, u_here, precision=highest)
        row_total = row_total + jnp.einsum("pi,pvn->ivn", row_hot, products, precision=highest)
        picked_w = jnp.einsum("pi,vin->pvn", row_hot, w_blocks, precision=highest)
        transposed = jnp.einsum("pkn,pvn->pvk", u_here, picked_w, precision=highest) * valid_mask[:, None, :]
        transposed = lax.optimization_barrier(transposed.astype(jnp.bfloat16)).astype(jnp.float32)
        returned = jnp.einsum("pvk,pkn->pvn", transposed, v_here, precision=highest)
        column_part = jnp.einsum("pb,pvn->vbn", col_hot, returned, precision=highest)
        column_parts.append(column_part.reshape(VECS, per_group * TILE))
    diag_blocks = x_blocks.reshape(VECS, col_count * per_group, TILE)[:, :row_count]
    dense_tiles = diag_tiles.astype(jnp.float32).reshape(row_count, TILE, TILE)
    diag_part = jnp.einsum("inm,vim->ivn", dense_tiles, diag_blocks, precision=highest)
    product_rows = (row_total + diag_part).astype(jnp.bfloat16).transpose(1, 0, 2).reshape(VECS, row_count * TILE)
    product_cols = jnp.concatenate(column_parts, axis=1).astype(jnp.bfloat16)
    return (product_rows, product_cols)
```

```python
import functools

import jax
import jax.numpy as jnp
from jax import lax
from jax.experimental import pallas as pl
from jax.experimental.pallas import tpu as pltpu
from jax.sharding import PartitionSpec as P

PANEL = 128
MESH = pl.DeviceIdType.MESH


def dot_nt(a, b):
    return lax.dot_general(a, b, (((1,), (1,)), ((), ())), preferred_element_type=jnp.float32)


def kernel(
    dims, ranks, order, x_hbm, w_hbm, diag_hbm, v_hbm, u_hbm, rows_out, cols_out,
    xg, wg, dvec, diag, v, u, row_ids, col_ids, lhs_rows, lhs_cols, p_rows, p_cols, sum3,
    col_sr, col_rr, col_sl, col_rl, s1, r1, s2, r2, s3, r3,
    load_sem, w_zr, w_zl, w_x, w_c, x_zr, x_zl, d_sem, c_zr, c_zl, r1_sem, r2_sem, r3_sem,
):
    R, C, V, W, Q, TILE, PG = dims
    X = C // 2
    total = v.shape[0]
    slots = total // PANEL
    grp, c, z = lax.axis_index("groups"), lax.axis_index("col"), lax.axis_index("row")
    mx, core = c // 2, c % 2
    sib = mx * 2 + (1 - core)
    row_of = lambda zz: (grp, c, zz)
    col_of = lambda cc: (grp, cc, z)
    sends = []

    def when(cond, fn):
        if cond is True:
            fn()
        else:
            pl.when(cond)(fn)

    def send(cond, make):
        when(cond, lambda: make().start())
        sends.append((cond, make))

    def rows_at(i):
        return pl.ds(pl.multiple_of(i * V, V), V)

    def lanes_at(i, n):
        return pl.ds(pl.multiple_of(i * n, n), n)

    def remote(src, dst, sems, dev):
        return pltpu.make_async_remote_copy(
            src_ref=src, dst_ref=dst, send_sem=sems[0], recv_sem=sems[1],
            device_id=dev, device_id_type=MESH,
        )

    def pair(sem, *index):
        return sem.at[(0, *index)], sem.at[(1, *index)]

    def x_slot(ref, r):
        return ref.at[rows_at(r * W // TILE), lanes_at(r % (TILE // W), W)]

    def w_slot(i, cc):
        return wg.at[rows_at(i), lanes_at(cc, Q)]

    load_x = pltpu.make_async_copy(x_hbm, x_slot(xg, z), load_sem.at[0])
    load_w = pltpu.make_async_copy(w_hbm, w_slot(z, c), load_sem.at[1])
    load_u = pltpu.make_async_copy(u_hbm, u, load_sem.at[2])
    load_v = pltpu.make_async_copy(v_hbm, v, load_sem.at[3])
    load_d = pltpu.make_async_copy(diag_hbm, diag, load_sem.at[4])
    for load in (load_w, load_x, load_u, load_v, load_d):
        load.start()

    barrier = pltpu.get_barrier_semaphore()
    for step in range(1, R):
        pl.semaphore_signal(barrier, inc=1, device_id=row_of((z + step) % R), device_id_type=MESH)
    for step in range(1, C):
        pl.semaphore_signal(barrier, inc=1, device_id=col_of((c + step) % C), device_id_type=MESH)
    pl.semaphore_wait(barrier, R + C - 2)

    def w_right(s):
        return remote(w_slot(z - s, c), w_slot(z - s, c), pair(w_zr, s), row_of(z + 1))

    def w_left(s):
        return remote(w_slot(z + s, c), w_slot(z + s, c), pair(w_zl, s), row_of(z - 1))

    def w_across(i, dx):
        return remote(w_slot(i, c), w_slot(i, c), pair(w_x, dx, i), col_of((mx + dx) % X * 2 + core))

    def w_sibling(i, dx):
        cc = (mx + dx) % X * 2 + core
        return remote(w_slot(i, cc), w_slot(i, cc), pair(w_c, dx, i), col_of(sib))

    def w_spread(cond, i):
        for dx in range(1, X):
            send(cond, lambda dx=dx: w_across(i, dx))
        send(cond, lambda: w_sibling(i, 0))

    def w_crossed(cond, i):
        for dx in range(1, X):
            cc = (mx - dx + X) % X * 2 + core
            arrived = lambda dx=dx, cc=cc: remote(
                w_slot(i, cc), w_slot(i, cc), pair(w_x, dx, i), col_of(c)).wait_recv()
            when(cond, arrived)
            send(cond, lambda dx=dx: w_sibling(i, X - dx))

    def x_right(s):
        return remote(x_slot(xg, z - s), x_slot(xg, z - s), pair(x_zr, s), row_of(z + 1))

    def x_left(s):
        return remote(x_slot(xg, z + s), x_slot(xg, z + s), pair(x_zl, s), row_of(z - 1))

    def x_send(s):
        send((z < R - 1) & (z >= s), lambda: x_right(s))
        send((z > 0) & (z + s < R), lambda: x_left(s))

    def x_wait(s):
        pl.when(z - 1 - s >= 0)(lambda: remote(
            x_slot(xg, z - 1 - s), x_slot(xg, z - 1 - s), pair(x_zr, s), row_of(z)).wait_recv())
        pl.when(z + 1 + s < R)(lambda: remote(
            x_slot(xg, z + 1 + s), x_slot(xg, z + 1 + s), pair(x_zl, s), row_of(z)).wait_recv())

    load_w.wait()
    send(z < R - 1, lambda: w_right(0))
    send(z > 0, lambda: w_left(0))
    w_spread(True, z)
    load_x.wait()
    x_send(0)

    lane = lax.broadcasted_iota(jnp.int32, (1, total), 1) + z * total
    in_row = jnp.full((1, total), -1, jnp.int32)
    in_col = jnp.full((1, total), -1, jnp.int32)
    start = jnp.int32(0)
    for p in range(R * PG):
        tile = order[0, p]
        ti, tj = tile // PG, tile % PG
        rank = jnp.where(ti == c * PG + tj, 0, ranks[ti, tj])
        offset = lane - start * PANEL
        hit = (offset >= 0) & (offset < rank)
        in_row = jnp.where(hit, ti, in_row)
        in_col = jnp.where(hit, tj, in_col)
        start = start + (rank + PANEL - 1) // PANEL
    row_ids[...] = in_row
    col_ids[...] = in_col

    for s in range(R - 1):
        from_left, from_right = z - 1 - s, z + 1 + s
        pl.when(from_left >= 0)(lambda: remote(
            w_slot(from_left, c), w_slot(from_left, c), pair(w_zr, s), row_of(z)).wait_recv())
        if s < R - 2:
            send((z < R - 1) & (from_left >= 0), lambda s=s: w_right(s + 1))
        w_spread(from_left >= 0, from_left)
        pl.when(from_right < R)(lambda: remote(
            w_slot(from_right, c), w_slot(from_right, c), pair(w_zl, s), row_of(z)).wait_recv())
        if s < R - 2:
            send((z > 0) & (from_right < R), lambda s=s: w_left(s + 1))
        w_spread(from_right < R, from_right)
        if s == 0:
            w_crossed(True, z)
        else:
            w_crossed(z - s >= 0, z - s)
            w_crossed(z + s < R, z + s)
    w_crossed(z - (R - 1) >= 0, z - (R - 1))
    w_crossed(z + (R - 1) < R, z + (R - 1))

    x_wait(0)
    if R > 2:
        x_send(1)

    root = z // PG
    diag_early = W == TILE and R <= PG

    def diag_send():
        for step in range(1, C):
            send(c == root, lambda step=step: remote(
                xg.at[rows_at(z % PG)], dvec, pair(d_sem, step), col_of((c + step) % C)))

    if diag_early:
        diag_send()

    for dx in range(X):
        cc = (mx + dx) % X * 2 + (1 - core)
        for i in range(R):
            remote(w_slot(i, cc), w_slot(i, cc), pair(w_c, dx, i), col_of(c)).wait_recv()

    def project(src, count, panels, ids, other_ids, lhs, other_count):
        width = 256 if total % 256 == 0 else PANEL

        def step(k, carry):
            lanes = lanes_at(k, width)
            res = dot_nt(src[...], panels[lanes, :])
            own, other = ids[:, lanes], other_ids[:, lanes]
            found = jnp.zeros((V, width), jnp.float32)
            for i in range(count):
                found = jnp.where(own == i, res[i * V:(i + 1) * V], found)
            for j in range(other_count):
                lhs[j * V:(j + 1) * V, lanes] = jnp.where(other == j, found, 0.0).astype(lhs.dtype)
            return carry

        lax.fori_loop(0, total // width, step, 0)

    def expand(lhs, panels, out):
        width = min(256, TILE)

        def step(k, carry):
            lanes = lanes_at(k, width)
            out[:, lanes] = jnp.dot(lhs[...], panels[:, lanes], preferred_element_type=jnp.float32)
            return carry

        lax.fori_loop(0, TILE // width, step, 0)

    load_u.wait()
    project(wg, R, u, row_ids, col_ids, lhs_cols, PG)
    load_v.wait()
    expand(lhs_cols, v, p_cols)

    def col_part(d):
        return p_cols[rows_at(d * W // TILE), lanes_at(d % (TILE // W), W)]

    def col_phase(k):
        t_right, t_left = k - z, k - (R - 1 - z)
        go_right, go_left = (z <= k) & (z < R - 1), (R - 1 - z <= k) & (z > 0)

        def right():
            return remote(col_sr.at[t_right], col_rr.at[t_right], pair(c_zr, t_right), row_of(z + 1))

        def left():
            return remote(col_sl.at[t_left], col_rl.at[t_left], pair(c_zl, t_left), row_of(z - 1))

        @pl.when(go_right & (z == 0))
        def _():
            col_sr[t_right] = col_part(R - 1 - t_right).astype(col_sr.dtype)

        @pl.when(go_right & (z > 0))
        def _():
            remote(col_sr.at[t_right], col_rr.at[t_right], pair(c_zr, t_right), row_of(z)).wait_recv()
            col_sr[t_right] = (col_part(R - 1 - t_right) + col_rr[t_right].astype(jnp.float32)).astype(col_sr.dtype)

        send(go_right, right)

        @pl.when(go_left & (z == R - 1))
        def _():
            col_sl[t_left] = col_part(t_left).astype(col_sl.dtype)

        @pl.when(go_left & (z < R - 1))
        def _():
            remote(col_sl.at[t_left], col_rl.at[t_left], pair(c_zl, t_left), row_of(z)).wait_recv()
            col_sl[t_left] = (col_part(t_left) + col_rl[t_left].astype(jnp.float32)).astype(col_sl.dtype)

        send(go_left, left)

    for k in range(R - 2):
        col_phase(k)
        x_wait(k + 1)
        if k + 2 < R - 1:
            x_send(k + 2)
    if R == 2:
        pass
    if not diag_early:
        diag_send()

    project(xg, PG, v, col_ids, row_ids, lhs_rows, R)
    expand(lhs_rows, u, p_rows)

    for dx in range(X):
        xx = (mx + dx) % X
        s1[dx] = p_rows[:, lanes_at(xx * 2 + 1 - core, Q)].astype(s1.dtype)
        send(True, lambda dx=dx: remote(s1.at[dx], r1.at[dx], pair(r1_sem, dx), col_of(sib)))

    col_phase(R - 2)

    for dx in list(range(1, X)) + [0]:
        remote(s1.at[dx], r1.at[dx], pair(r1_sem, dx), col_of(c)).wait_recv()
        xx = (mx + dx) % X
        part = p_rows[:, lanes_at(xx * 2 + core, Q)] + r1[dx].astype(jnp.float32)
        if dx:
            s2[dx] = part.astype(s2.dtype)
            send(True, lambda dx=dx, xx=xx: remote(
                s2.at[dx], r2.at[dx], pair(r2_sem, dx), col_of(xx * 2 + core)))
        else:
            sum3[...] = part

    load_d.wait()
    pl.when(c == root)(lambda: dvec.__setitem__(..., xg[rows_at(z % PG)]))
    for step in range(1, C):
        pl.when((c != root) & (c == (root + step) % C))(lambda step=step: remote(
            dvec, dvec, pair(d_sem, step), col_of(c)).wait_recv())
    diag_part = dot_nt(dvec[...], diag[...])

    for dx in range(1, X):
        remote(s2.at[dx], r2.at[dx], pair(r2_sem, dx), col_of(c)).wait_recv()
        sum3[...] += r2[dx].astype(jnp.float32)
    s3[...] = sum3[...].astype(s3.dtype)
    for step in range(1, R):
        to = (z + step) % R
        send(True, lambda step=step, to=to: remote(
            s3.at[rows_at(to)], r3.at[rows_at(step)], pair(r3_sem, step), row_of(to)))

    result = col_part(z)
    cols_out[...] = result.astype(cols_out.dtype)
    acc = p_cols.at[rows_at(z * W // TILE), lanes_at(z % (TILE // W), W)]

    @pl.when(z > 0)
    def _():
        t = R - 1 - z
        remote(col_sr.at[t], col_rr.at[t], pair(c_zr, t), row_of(z)).wait_recv()
        acc[...] += col_rr[t].astype(jnp.float32)

    @pl.when(z < R - 1)
    def _():
        remote(col_sl.at[z], col_rl.at[z], pair(c_zl, z), row_of(z)).wait_recv()
        acc[...] += col_rl[z].astype(jnp.float32)

    cols_out[...] = acc[...].astype(cols_out.dtype)

    out = sum3[rows_at(z)] + diag_part
    for step in range(1, R):
        remote(s3.at[rows_at(0)], r3.at[rows_at(step)], pair(r3_sem, step), row_of(z)).wait_recv()
        out = out + r3[rows_at(step)].astype(jnp.float32)
    rows_out[...] = out.astype(rows_out.dtype)

    for cond, make in sends:
        when(cond, lambda make=make: make().wait_send())


def body(mesh_shape, right_vectors, left_vectors, diag_tiles, tile_ranks, tile_order, v_panels, u_panels):
    R, C = mesh_shape["row"], mesh_shape["col"]
    X = C // 2
    V, W = right_vectors.shape
    Q = left_vectors.shape[1]
    TILE = diag_tiles.shape[1]
    PG = tile_ranks.shape[1]
    total = v_panels.shape[0] * PANEL
    b16, f32 = jnp.bfloat16, jnp.float32
    any_spec = pl.BlockSpec(memory_space=pl.ANY)
    smem = pl.BlockSpec(memory_space=pltpu.SMEM)
    vmem = pl.BlockSpec(memory_space=pltpu.VMEM)
    dma = pltpu.SemaphoreType.DMA
    steps = R - 1
    return pl.pallas_call(
        functools.partial(kernel, (R, C, V, W, Q, TILE, PG)),
        out_shape=(
            jax.ShapeDtypeStruct((V, Q), b16),
            jax.ShapeDtypeStruct((V, W), b16),
        ),
        in_specs=[smem, smem] + [any_spec] * 5,
        out_specs=(vmem, vmem),
        scratch_shapes=[
            pltpu.VMEM((PG * V, TILE), b16),
            pltpu.VMEM((R * V, TILE), b16),
            pltpu.VMEM((V, TILE), b16),
            pltpu.VMEM((Q, TILE), b16),
            pltpu.VMEM((total, TILE), b16),
            pltpu.VMEM((total, TILE), b16),
            pltpu.VMEM((1, total), jnp.int32),
            pltpu.VMEM((1, total), jnp.int32),
            pltpu.VMEM((R * V, total), b16),
            pltpu.VMEM((PG * V, total), b16),
            pltpu.VMEM((R * V, TILE), f32),
            pltpu.VMEM((PG * V, TILE), f32),
            pltpu.VMEM((R * V, Q), f32),
            pltpu.VMEM((steps, V, W), b16),
            pltpu.VMEM((steps, V, W), b16),
            pltpu.VMEM((steps, V, W), b16),
            pltpu.VMEM((steps, V, W), b16),
            pltpu.VMEM((X, R * V, Q), b16),
            pltpu.VMEM((X, R * V, Q), b16),
            pltpu.VMEM((X, R * V, Q), b16),
            pltpu.VMEM((X, R * V, Q), b16),
            pltpu.VMEM((R * V, Q), b16),
            pltpu.VMEM((R * V, Q), b16),
            dma((5,)),
            dma((2, steps)),
            dma((2, steps)),
            dma((2, X, R)),
            dma((2, X, R)),
            dma((2, steps)),
            dma((2, steps)),
            dma((2, C)),
            dma((2, steps)),
            dma((2, steps)),
            dma((2, X)),
            dma((2, X)),
            dma((2, R)),
        ],
        compiler_params=pltpu.CompilerParams(
            collective_id=0, has_side_effects=True, vmem_limit_bytes=48 * 1024 * 1024
        ),
        name="slab",
    )(
        tile_ranks, tile_order, right_vectors, left_vectors, diag_tiles,
        v_panels.reshape(total, TILE), u_panels.reshape(total, TILE),
    )


def solution(mesh):
    in_specs = (
        P("groups", ("col", "row")),
        P("groups", ("row", "col")),
        P(("groups", "row", "col"), None),
        P("groups", "col"),
        P(("groups", "col"), None),
        P(("groups", "col", "row"), None, None),
        P(("groups", "col", "row"), None, None),
    )
    out_specs = (P("groups", ("row", "col")), P("groups", ("col", "row")))
    return jax.shard_map(
        functools.partial(body, dict(mesh.shape)),
        mesh=mesh, in_specs=in_specs, out_specs=out_specs, check_vma=False,
    )
```

```python
import functools

import jax
import jax.numpy as jnp
from jax import lax
from jax.experimental import pallas as pl
from jax.experimental.pallas import tpu as pltpu
from jax.sharding import PartitionSpec as P

PANEL = 128
HALVES = 2
MESH = pl.DeviceIdType.MESH


def dot_nt(a, b):
    return lax.dot_general(a, b, (((1,), (1,)), ((), ())), preferred_element_type=jnp.float32)


def kernel(
    dims, ranks, order, x_hbm, w_hbm, diag_hbm, v_hbm, u_hbm, rows_out, cols_out,
    xg, wg, dvec, diag, v, u, row_ids, col_ids, lhs_rows, lhs_cols, p_rows, p_cols, sum3,
    col_sr, col_rr, col_sl, col_rl, s1, r1, s2, r2, s3, r3,
    load_sem, w_zr, w_zl, w_x, w_c, x_zr, x_zl, d_sem, c_zr, c_zl, r1_sem, r2_sem, r3_sem,
):
    R, C, V, W, Q, TILE, PG = dims
    X = C // 2
    total = v.shape[0]
    H = V // HALVES
    grp, c, z = lax.axis_index("groups"), lax.axis_index("col"), lax.axis_index("row")
    mx, core = c // 2, c % 2
    sib = mx * 2 + (1 - core)
    row_of = lambda zz: (grp, c, zz)
    col_of = lambda cc: (grp, cc, z)
    sends = []

    def when(cond, fn):
        if cond is True:
            fn()
        else:
            pl.when(cond)(fn)

    def send(cond, make):
        when(cond, lambda: make().start())
        sends.append((cond, make))

    def rows_at(i):
        return pl.ds(pl.multiple_of(i * V, V), V)

    def lanes_at(i, n):
        return pl.ds(pl.multiple_of(i * n, n), n)

    def remote(src, dst, sems, dev):
        return pltpu.make_async_remote_copy(
            src_ref=src, dst_ref=dst, send_sem=sems[0], recv_sem=sems[1],
            device_id=dev, device_id_type=MESH,
        )

    def pair(sem, *index):
        return sem.at[(0, *index)], sem.at[(1, *index)]

    def x_slot(ref, r, h=None):
        lanes = lanes_at(r % (TILE // W), W)
        if h is None:
            return ref.at[rows_at(r * W // TILE), lanes]
        return ref.at[pl.ds(pl.multiple_of(r * W // TILE * V + h * H, H), H), lanes]

    def w_slot(i, cc):
        return wg.at[rows_at(i), lanes_at(cc, Q)]

    load_x = pltpu.make_async_copy(x_hbm, x_slot(xg, z), load_sem.at[0])
    load_w = pltpu.make_async_copy(w_hbm, w_slot(z, c), load_sem.at[1])
    load_u = pltpu.make_async_copy(u_hbm, u, load_sem.at[2])
    load_v = pltpu.make_async_copy(v_hbm, v, load_sem.at[3])
    load_d = pltpu.make_async_copy(diag_hbm, diag, load_sem.at[4])
    for load in (load_w, load_x, load_u, load_v, load_d):
        load.start()

    barrier = pltpu.get_barrier_semaphore()
    for step in range(1, R):
        pl.semaphore_signal(barrier, inc=1, device_id=row_of((z + step) % R), device_id_type=MESH)
    for step in range(1, C):
        pl.semaphore_signal(barrier, inc=1, device_id=col_of((c + step) % C), device_id_type=MESH)
    pl.semaphore_wait(barrier, R + C - 2)

    def w_right(s):
        return remote(w_slot(z, c), w_slot(z, c), pair(w_zr, s), row_of(z + 1 + s))

    def w_left(s):
        return remote(w_slot(z, c), w_slot(z, c), pair(w_zl, s), row_of(z - 1 - s))

    def w_across(i, dx):
        return remote(w_slot(i, c), w_slot(i, c), pair(w_x, dx, i), col_of((mx + dx) % X * 2 + core))

    def w_sibling(i, dx):
        cc = (mx + dx) % X * 2 + core
        return remote(w_slot(i, cc), w_slot(i, cc), pair(w_c, dx, i), col_of(sib))

    def w_spread(cond, i):
        for dx in range(1, X):
            send(cond, lambda dx=dx: w_across(i, dx))
        send(cond, lambda: w_sibling(i, 0))

    def w_crossed(cond, i):
        for dx in range(1, X):
            cc = (mx - dx + X) % X * 2 + core
            arrived = lambda dx=dx, cc=cc: remote(
                w_slot(i, cc), w_slot(i, cc), pair(w_x, dx, i), col_of(c)).wait_recv()
            when(cond, arrived)
            send(cond, lambda dx=dx: w_sibling(i, X - dx))

    def x_half(r, h):
        return x_slot(xg, r, h)

    def x_right(s, h):
        return remote(x_half(z - s, h), x_half(z - s, h), pair(x_zr, s, h), row_of(z + 1))

    def x_left(s, h):
        return remote(x_half(z + s, h), x_half(z + s, h), pair(x_zl, s, h), row_of(z - 1))

    def x_send(s, h):
        send((z < R - 1) & (z >= s), lambda: x_right(s, h))
        send((z > 0) & (z + s < R), lambda: x_left(s, h))

    def x_wait(s, h):
        left, right = z - 1 - s, z + 1 + s
        pl.when(left >= 0)(lambda: remote(
            x_half(left, h), x_half(left, h), pair(x_zr, s, h), row_of(z)).wait_recv())
        pl.when(right < R)(lambda: remote(
            x_half(right, h), x_half(right, h), pair(x_zl, s, h), row_of(z)).wait_recv())

    def x_pass(s):
        for h in range(HALVES):
            x_wait(s, h)
            if s + 1 < R - 1:
                x_send(s + 1, h)

    load_w.wait()
    for s in range(R - 1):
        send(z + 1 + s < R, lambda s=s: w_right(s))
        send(z - 1 - s >= 0, lambda s=s: w_left(s))
    w_spread(True, z)
    load_x.wait()
    for h in range(HALVES):
        x_send(0, h)

    lane = lax.broadcasted_iota(jnp.int32, (1, total), 1) + z * total
    in_row = jnp.full((1, total), -1, jnp.int32)
    in_col = jnp.full((1, total), -1, jnp.int32)
    start = jnp.int32(0)
    for p in range(R * PG):
        tile = order[0, p]
        ti, tj = tile // PG, tile % PG
        rank = jnp.where(ti == c * PG + tj, 0, ranks[ti, tj])
        offset = lane - start * PANEL
        hit = (offset >= 0) & (offset < rank)
        in_row = jnp.where(hit, ti, in_row)
        in_col = jnp.where(hit, tj, in_col)
        start = start + (rank + PANEL - 1) // PANEL
    row_ids[...] = in_row
    col_ids[...] = in_col

    for s in range(R - 1):
        from_left, from_right = z - 1 - s, z + 1 + s
        pl.when(from_left >= 0)(lambda: remote(
            w_slot(from_left, c), w_slot(from_left, c), pair(w_zr, s), row_of(z)).wait_recv())
        w_spread(from_left >= 0, from_left)
        pl.when(from_right < R)(lambda: remote(
            w_slot(from_right, c), w_slot(from_right, c), pair(w_zl, s), row_of(z)).wait_recv())
        w_spread(from_right < R, from_right)
        if s == 0:
            w_crossed(True, z)
        else:
            w_crossed(z - s >= 0, z - s)
            w_crossed(z + s < R, z + s)
    w_crossed(z - (R - 1) >= 0, z - (R - 1))
    w_crossed(z + (R - 1) < R, z + (R - 1))

    x_pass(0)

    root = z // PG
    diag_early = W == TILE and R <= PG

    def diag_send():
        for step in range(1, C):
            send(c == root, lambda step=step: remote(
                xg.at[rows_at(z % PG)], dvec, pair(d_sem, step), col_of((c + step) % C)))

    if diag_early:
        diag_send()

    for dx in range(X):
        cc = (mx + dx) % X * 2 + (1 - core)
        for i in range(R):
            remote(w_slot(i, cc), w_slot(i, cc), pair(w_c, dx, i), col_of(c)).wait_recv()

    def project(src, count, panels, ids, other_ids, lhs, other_count):
        width = 256 if total % 256 == 0 else PANEL

        def step(k, carry):
            lanes = lanes_at(k, width)
            res = dot_nt(src[...], panels[lanes, :])
            own, other = ids[:, lanes], other_ids[:, lanes]
            found = jnp.zeros((V, width), jnp.float32)
            for i in range(count):
                found = jnp.where(own == i, res[i * V:(i + 1) * V], found)
            for j in range(other_count):
                lhs[j * V:(j + 1) * V, lanes] = jnp.where(other == j, found, 0.0).astype(lhs.dtype)
            return carry

        lax.fori_loop(0, total // width, step, 0)

    def expand(lhs, panels, out, first, count):
        width = min(256, count)

        def step(k, carry):
            lanes = pl.ds(pl.multiple_of(first + k * width, width), width)
            out[:, lanes] = jnp.dot(lhs[...], panels[:, lanes], preferred_element_type=jnp.float32)
            return carry

        lax.fori_loop(0, count // width, step, 0)

    load_u.wait()
    if R > 2:
        x_pass(1)
    project(wg, R, u, row_ids, col_ids, lhs_cols, PG)
    load_v.wait()
    expand(lhs_cols, v, p_cols, 0, TILE)

    def col_slot(d, h=None):
        lanes = lanes_at(d % (TILE // W), W)
        if h is None:
            return p_cols.at[rows_at(d * W // TILE), lanes]
        return p_cols.at[pl.ds(pl.multiple_of(d * W // TILE * V + h * H, H), H), lanes]

    def col_phase(k, h):
        t_right, t_left = k - z, k - (R - 1 - z)
        go_right, go_left = (z <= k) & (z < R - 1), (R - 1 - z <= k) & (z > 0)
        half = pl.ds(h * H, H)

        def one(go, first, t, d, out, into, sem, dev):
            def make(to):
                return remote(out.at[t, half], into.at[t, half], pair(sem, t, h), to)

            @pl.when(go & first)
            def _():
                out[t, half] = col_slot(d, h)[...].astype(out.dtype)

            @pl.when(go & jnp.logical_not(first))
            def _():
                make(row_of(z)).wait_recv()
                out[t, half] = (col_slot(d, h)[...] + into[t, half].astype(jnp.float32)).astype(out.dtype)

            send(go, lambda: make(row_of(dev)))

        one(go_right, z == 0, t_right, R - 1 - t_right, col_sr, col_rr, c_zr, z + 1)
        one(go_left, z == R - 1, t_left, t_left, col_sl, col_rl, c_zl, z - 1)

    def col_step(k):
        for h in range(HALVES):
            col_phase(k, h)

    for k in range(R - 3):
        col_step(k)
        x_pass(k + 2)
    if not diag_early:
        diag_send()

    project(xg, PG, v, col_ids, row_ids, lhs_rows, R)
    others = [(mx + dx) % X for dx in range(1, X)]

    def row_send(dx, xx):
        lanes = lanes_at(xx * 2 + 1 - core, Q)
        expand(lhs_rows, u, p_rows, lanes.start, Q)
        s1[dx] = p_rows[:, lanes].astype(s1.dtype)
        send(True, lambda: remote(s1.at[dx], r1.at[dx], pair(r1_sem, dx), col_of(sib)))

    def row_wait(dx):
        remote(s1.at[dx], r1.at[dx], pair(r1_sem, dx), col_of(c)).wait_recv()

    def across(dx, step, to):
        rows = rows_at((z + step) % R)
        return remote(s2.at[dx, rows], r2.at[dx, rows], pair(r2_sem, dx, step), to)

    for dx, xx in enumerate(others, 1):
        row_send(dx, xx)
    for dx, xx in enumerate(others, 1):
        expand(lhs_rows, u, p_rows, (xx * 2 + core) * Q, Q)
    if R > 2:
        col_step(R - 3)
    for dx, xx in enumerate(others, 1):
        row_wait(dx)
        for step in list(range(1, R)) + [0]:
            rows = rows_at((z + step) % R)
            s2[dx, rows] = (
                p_rows[rows, lanes_at(xx * 2 + core, Q)] + r1[dx, rows].astype(jnp.float32)
            ).astype(s2.dtype)
            send(True, lambda dx=dx, xx=xx, step=step: across(dx, step, col_of(xx * 2 + core)))
    row_send(0, mx)
    expand(lhs_rows, u, p_rows, c * Q, Q)
    col_step(R - 2)
    row_wait(0)
    sum3[...] = p_rows[:, lanes_at(c, Q)] + r1[0].astype(jnp.float32)

    load_d.wait()
    pl.when(c == root)(lambda: dvec.__setitem__(..., xg[rows_at(z % PG)]))
    for step in range(1, C):
        pl.when((c != root) & (c == (root + step) % C))(lambda step=step: remote(
            dvec, dvec, pair(d_sem, step), col_of(c)).wait_recv())
    diag_part = dot_nt(dvec[...], diag[...])

    for step in list(range(1, R)) + [0]:
        to = (z + step) % R
        rows = rows_at(to)
        for dx in range(1, X):
            across(dx, step, col_of(c)).wait_recv()
            sum3[rows] += r2[dx, rows].astype(jnp.float32)
        if step:
            s3[rows] = sum3[rows].astype(s3.dtype)
            send(True, lambda step=step, to=to, rows=rows: remote(
                s3.at[rows], r3.at[rows_at(step)], pair(r3_sem, step), row_of(to)))

    acc = col_slot(z)
    for h in range(HALVES):
        half = pl.ds(h * H, H)

        def last(t, out, into, sem):
            remote(out.at[t, half], into.at[t, half], pair(sem, t, h), row_of(z)).wait_recv()
            col_slot(z, h)[...] += into[t, half].astype(jnp.float32)

        pl.when(z > 0)(lambda: last(R - 1 - z, col_sr, col_rr, c_zr))
        pl.when(z < R - 1)(lambda: last(z, col_sl, col_rl, c_zl))
    cols_out[...] = acc[...].astype(cols_out.dtype)

    out = sum3[rows_at(z)] + diag_part
    for step in range(1, R):
        remote(s3.at[rows_at(0)], r3.at[rows_at(step)], pair(r3_sem, step), row_of(z)).wait_recv()
        out = out + r3[rows_at(step)].astype(jnp.float32)
    rows_out[...] = out.astype(rows_out.dtype)

    for cond, make in sends:
        when(cond, lambda make=make: make().wait_send())


def body(mesh_shape, right_vectors, left_vectors, diag_tiles, tile_ranks, tile_order, v_panels, u_panels):
    R, C = mesh_shape["row"], mesh_shape["col"]
    X = C // 2
    V, W = right_vectors.shape
    Q = left_vectors.shape[1]
    TILE = diag_tiles.shape[1]
    PG = tile_ranks.shape[1]
    total = v_panels.shape[0] * PANEL
    b16, f32 = jnp.bfloat16, jnp.float32
    any_spec = pl.BlockSpec(memory_space=pl.ANY)
    smem = pl.BlockSpec(memory_space=pltpu.SMEM)
    vmem = pl.BlockSpec(memory_space=pltpu.VMEM)
    dma = pltpu.SemaphoreType.DMA
    steps = R - 1
    return pl.pallas_call(
        functools.partial(kernel, (R, C, V, W, Q, TILE, PG)),
        out_shape=(
            jax.ShapeDtypeStruct((V, Q), b16),
            jax.ShapeDtypeStruct((V, W), b16),
        ),
        in_specs=[smem, smem] + [any_spec] * 5,
        out_specs=(vmem, vmem),
        scratch_shapes=[
            pltpu.VMEM((PG * V, TILE), b16),
            pltpu.VMEM((R * V, TILE), b16),
            pltpu.VMEM((V, TILE), b16),
            pltpu.VMEM((Q, TILE), b16),
            pltpu.VMEM((total, TILE), b16),
            pltpu.VMEM((total, TILE), b16),
            pltpu.VMEM((1, total), jnp.int32),
            pltpu.VMEM((1, total), jnp.int32),
            pltpu.VMEM((R * V, total), b16),
            pltpu.VMEM((PG * V, total), b16),
            pltpu.VMEM((R * V, TILE), f32),
            pltpu.VMEM((PG * V, TILE), f32),
            pltpu.VMEM((R * V, Q), f32),
            pltpu.VMEM((steps, V, W), b16),
            pltpu.VMEM((steps, V, W), b16),
            pltpu.VMEM((steps, V, W), b16),
            pltpu.VMEM((steps, V, W), b16),
            pltpu.VMEM((X, R * V, Q), b16),
            pltpu.VMEM((X, R * V, Q), b16),
            pltpu.VMEM((X, R * V, Q), b16),
            pltpu.VMEM((X, R * V, Q), b16),
            pltpu.VMEM((R * V, Q), b16),
            pltpu.VMEM((R * V, Q), b16),
            dma((5,)),
            dma((2, steps)),
            dma((2, steps)),
            dma((2, X, R)),
            dma((2, X, R)),
            dma((2, steps, HALVES)),
            dma((2, steps, HALVES)),
            dma((2, C)),
            dma((2, steps, HALVES)),
            dma((2, steps, HALVES)),
            dma((2, X)),
            dma((2, X, R)),
            dma((2, R)),
        ],
        compiler_params=pltpu.CompilerParams(
            collective_id=0, has_side_effects=True, vmem_limit_bytes=60 * 1024 * 1024
        ),
        name="slab",
    )(
        tile_ranks, tile_order, right_vectors, left_vectors, diag_tiles,
        v_panels.reshape(total, TILE), u_panels.reshape(total, TILE),
    )


def solution(mesh):
    in_specs = (
        P("groups", ("col", "row")),
        P("groups", ("row", "col")),
        P(("groups", "row", "col"), None),
        P("groups", "col"),
        P(("groups", "col"), None),
        P(("groups", "col", "row"), None, None),
        P(("groups", "col", "row"), None, None),
    )
    out_specs = (P("groups", ("row", "col")), P("groups", ("col", "row")))
    return jax.shard_map(
        functools.partial(body, dict(mesh.shape)),
        mesh=mesh, in_specs=in_specs, out_specs=out_specs, check_vma=False,
    )
```
